32 devices in a mesh: gx: 2 (over core), gy: 4 (over y, x), gz: 4 (over z).
Axes of the slice: x: 2, y: 2, z: 4, core: 2. Of those that a mesh axis runs over, the one named last changes fastest.
Arguments:
- edge_state: bfloat16 [65536, 512], P(('gx', 'gy', 'gz')), may hold values from -6 to 6
- angle_weight: float32 [65536, 32], P(('gx', 'gy', 'gz')), may hold values from -6 to 6
- angle_bins: int32 [65536, 32], P(('gx', 'gy', 'gz')), may hold values from 0 to 15
- send_slots: int32 [2, 4, 4, 27, 32], P('gx', 'gy', 'gz'), may hold values from -1 to 2047, as said below
- fetch_index: int32 [65536], P(('gx', 'gy', 'gz')), may hold values from -1 to 2911, as said below
- down_weight: bfloat16 [2, 512, 64], replicated, may hold values from -0.25 to 0.25
- bilinear: bfloat16 [2, 1024, 64], replicated, may hold values from -0.1875 to 0.1875
- up_weight: bfloat16 [2, 64, 512], replicated, may hold values from -0.75 to 0.75
- first_dense: bfloat16 [2, 512, 512], replicated, may hold values from -0.25 to 0.25
- second_dense: bfloat16 [2, 512, 512], replicated, may hold values from -0.25 to 0.25
Outputs:
- edge_out: bfloat16 [65536, 512], P(('gx', 'gy', 'gz'))
The draws below stay inside these ranges and needn't reach their ends.
Inputs may be any that keep to these rules, and one draw needn't show every extreme that they name: `send_slots`: direction t = 9a + 3b + c stands for the neighbouring brick at offset (a - 1, b - 1, c - 1), periodic. Row t of a brick lists, in its first slots, local edges whose reverses lie in the brick at direction t; the rest hold -1; row 13 holds only -1. Every edge is listed at most once. Some direction of every brick is full. `fetch_index`: -1 marks an empty neighbour slot. A value below 2048 is the local edge that is the reverse; 2048 + t * 32 + r says that the reverse is listed in slot r of row 26 - t of send_slots of the brick at direction t, and that this brick's own edge is listed in slot r of row t of its own send_slots. Reverses are mutual, live edges have live reverses, and rev of an edge is another edge.
All inputs are finite; a program needn't handle non-finite values.
Results may differ from the reference program's by a relative error of at most 0.014.
Values may be sent and summed in bfloat16 or wider, within the bound.
A program may use at most 128 MiB of HBM per device.

```python
from functools import partial
import jax
import jax.numpy as jnp
from jax import lax

D = 512
TRIP = 64
ANG = 16
NEIGH = 32
BLOCKS = 2
ATOMS_DEV = 64
EDGE_DEV = 2048
SLOTS = 32
BX = 2
BY = 4
BZ = 4
BRICKS = 32
EDGES = 65536


def graph_tables(key):
    base_key = jax.random.fold_in(key, 91)
    key_counts, key_self, key_order = jax.random.split(base_key, 3)
    bricks = BX * BY * BZ
    brick_id = jnp.arange(bricks, dtype=jnp.int32)
    direction = jnp.arange(27, dtype=jnp.int32)
    drawn_counts = jax.random.randint(key_counts, (bricks, 27), SLOTS // 4, SLOTS + 1, dtype=jnp.int32)
    drawn_counts = jnp.where(direction[None, :] == (brick_id % 13)[:, None], SLOTS, drawn_counts)
    coord_x = brick_id // (BY * BZ)
    coord_y = brick_id // BZ % BY
    coord_z = brick_id % BZ
    partner = ((coord_x[:, None] + direction[None, :] // 9 - 1) % BX * BY + (coord_y[:, None] + direction[None, :] // 3 % 3 - 1) % BY) * BZ + (coord_z[:, None] + direction[None, :] % 3 - 1) % BZ
    mirrored = drawn_counts[partner, 26 - direction[None, :]]
    inside = 2 * jax.random.randint(key_self, (bricks,), EDGE_DEV // 8, EDGE_DEV // 4 + 1, dtype=jnp.int32)
    counts = jnp.where(direction[None, :] < 13, drawn_counts, mirrored)
    counts = jnp.where(direction[None, :] == 13, inside[:, None], counts)
    starts = jnp.cumsum(counts, axis=1) - counts
    finish = starts + counts
    shuffled = jax.vmap(lambda sub_key: jax.random.permutation(sub_key, EDGE_DEV))(jax.random.split(key_order, bricks)).astype(jnp.int32)
    slot_rank = jnp.arange(SLOTS, dtype=jnp.int32)
    places = starts[:, :, None] + slot_rank[None, None, :]
    filled = (slot_rank[None, None, :] < counts[:, :, None]) & (direction[None, :, None] != 13)
    picked = jnp.take_along_axis(shuffled, jnp.clip(places, 0, EDGE_DEV - 1).reshape(bricks, 27 * SLOTS), axis=1).reshape(bricks, 27, SLOTS)
    send_table = jnp.where(filled, picked, -1)
    position = jnp.arange(EDGE_DEV, dtype=jnp.int32)
    group_of = jnp.sum((finish[:, None, :] <= position[None, :, None]).astype(jnp.int32), axis=2)
    group_safe = jnp.minimum(group_of, 26)
    offset = position[None, :] - jnp.take_along_axis(starts, group_safe, axis=1)
    partner_place = starts[:, 13][:, None] + jnp.bitwise_xor(offset, 1)
    local_pair = jnp.take_along_axis(shuffled, jnp.clip(partner_place, 0, EDGE_DEV - 1), axis=1)
    fetched = jnp.where(group_of == 13, local_pair, EDGE_DEV + group_safe * SLOTS + offset)
    fetched = jnp.where(group_of >= 27, -1, fetched)
    inverse = jnp.argsort(shuffled, axis=1)
    fetch_table = jnp.take_along_axis(fetched, inverse, axis=1)
    return (send_table.reshape(BX, BY, BZ, 27, SLOTS).astype(jnp.int32), fetch_table.reshape(bricks * EDGE_DEV).astype(jnp.int32))


def draw_send_slots(key, part):
    return graph_tables(key)[0]


def draw_fetch_index(key, part):
    return graph_tables(key)[1]


def touch_ends(drawn, stream_key, smallest, top_value):
    index_at = [jax.random.randint(jax.random.fold_in(stream_key, axis), (), 0, length) for axis, length in enumerate(drawn.shape)]
    longest = drawn.shape.index(max(drawn.shape))
    neighbour = index_at[:longest] + [(index_at[longest] + 1) % drawn.shape[longest]] + index_at[longest + 1:]
    return drawn.at[tuple(index_at)].set(smallest).at[tuple(neighbour)].set(top_value)


def block_levels(rng, extent, shards, smallest, top_value):
    def one(dim, parts):
        heights = jax.random.uniform(jax.random.fold_in(jax.random.fold_in(rng, 6), dim), (parts,), jnp.float32, smallest / len(shards), top_value / len(shards))
        return jnp.repeat(jnp.exp(heights), extent[dim] // parts).reshape((-1,) + (1,) * (len(extent) - dim - 1))

    level = one(*shards[0])
    for cut in shards[1:]:
        level = level * one(*cut)
    return level


def gaussian(rng, shape, spread, most, cuts=(), kind=jnp.bfloat16):
    gain = block_levels(rng, shape, cuts, -0.22, 0.18) if cuts else 1.0
    values = jax.random.normal(rng, shape, jnp.float32) * spread * gain
    return jnp.minimum(jnp.maximum(values, -most), most).astype(kind)


def setup_inputs(seed: int = 0) -> dict:
    keys = jax.random.split(jax.random.key(seed), 11)
    return {
        "edge_state": gaussian(keys[0], (EDGES, D), 1.0, 6.0, ((0, 32),)),
        "angle_weight": gaussian(keys[1], (EDGES, NEIGH), 1.0, 6.0, ((0, 32),), jnp.float32),
        "angle_bins": touch_ends(jax.random.randint(keys[2], (EDGES, NEIGH), 0, ANG), jax.random.fold_in(keys[2], 1), 0, ANG - 1).astype(jnp.int32),
        "send_slots": draw_send_slots(jax.random.fold_in(keys[10], 71), 0),
        "fetch_index": draw_fetch_index(jax.random.fold_in(keys[10], 71), 0),
        "down_weight": gaussian(keys[5], (BLOCKS, D, TRIP), D ** -0.5, 0.25),
        "bilinear": gaussian(keys[6], (BLOCKS, ANG * TRIP, TRIP), (ANG * TRIP) ** -0.5, 0.1875),
        "up_weight": gaussian(keys[7], (BLOCKS, TRIP, D), TRIP ** -0.5, 0.75),
        "first_dense": gaussian(keys[8], (BLOCKS, D, D), D ** -0.5, 0.25),
        "second_dense": gaussian(keys[9], (BLOCKS, D, D), D ** -0.5, 0.25),
    }


HALF_ROOT = 0.7071067811865476


def reverse_table(send_slots, fetch_index):
    senders = send_slots.reshape(BRICKS, 27, SLOTS)
    position = jnp.arange(EDGES, dtype=jnp.int32)
    brick_id = position // EDGE_DEV
    remote = jnp.maximum(fetch_index - EDGE_DEV, 0)
    direction = remote // SLOTS
    within = remote % SLOTS
    coord_x = brick_id // (BY * BZ)
    coord_y = (brick_id // BZ) % BY
    coord_z = brick_id % BZ
    source = (((coord_x + direction // 9 - 1) % BX) * BY + (coord_y + (direction // 3) % 3 - 1) % BY) * BZ + (coord_z + direction % 3 - 1) % BZ
    distant = source * EDGE_DEV + senders[source, 26 - direction, within]
    nearby = brick_id * EDGE_DEV + jnp.maximum(fetch_index, 0)
    reverse = jnp.where(fetch_index >= EDGE_DEV, distant, nearby).astype(jnp.int32)
    return reverse, fetch_index >= 0


def per_brick(function, *arrays):
    shaped = tuple(array.reshape((BRICKS, EDGE_DEV) + array.shape[1:]) for array in arrays)
    result = lax.map(lambda pieces: function(*pieces), shaped)
    return result.reshape((EDGES,) + result.shape[2:])


def fetch_rows(values, reverse, live_edge):
    return jnp.where(live_edge[:, None], values[reverse], jnp.zeros((), values.dtype))


def project_down(row_block, down_l):
    return jax.nn.silu(jnp.dot(row_block, down_l, preferred_element_type=jnp.float32)).astype(jnp.bfloat16)


def triplets(gathered, weight_rows, bin_rows, live_rows, bilinear_l, up_l):
    neighbours = gathered.reshape(ATOMS_DEV, NEIGH, TRIP).astype(jnp.float32)
    slot_ids = jnp.arange(NEIGH, dtype=jnp.int32)
    distinct = slot_ids[:, None] != slot_ids[None, :]
    kept_pairs = live_rows.reshape(ATOMS_DEV, 1, NEIGH) & distinct[None]
    chosen = bin_rows.reshape(ATOMS_DEV, NEIGH, NEIGH)[..., None] == jnp.arange(ANG, dtype=jnp.int32)
    coefficients = jnp.where(kept_pairs[..., None] & chosen, weight_rows.reshape(ATOMS_DEV, NEIGH, NEIGH)[..., None], jnp.float32(0.0)).astype(jnp.bfloat16)
    summed = jnp.einsum("akjb,ajc->akbc", coefficients.astype(jnp.float32), neighbours)
    summed = summed.astype(jnp.bfloat16).reshape(EDGE_DEV, ANG * TRIP)
    triplet_out = jnp.dot(summed, bilinear_l, preferred_element_type=jnp.float32).astype(jnp.bfloat16)
    return jax.nn.silu(jnp.dot(triplet_out, up_l, preferred_element_type=jnp.float32)).astype(jnp.bfloat16)


def residual(row_block, returned, live_rows, first_l, second_l):
    mixed_rows = ((row_block.astype(jnp.float32) + returned.astype(jnp.float32)) * HALF_ROOT).astype(jnp.bfloat16)
    inner_rows = jax.nn.silu(jnp.dot(mixed_rows, first_l, preferred_element_type=jnp.float32)).astype(jnp.bfloat16)
    updated = (mixed_rows.astype(jnp.float32) + jax.nn.silu(jnp.dot(inner_rows, second_l, preferred_element_type=jnp.float32))) * HALF_ROOT
    return jnp.where(live_rows[:, None], updated, jnp.float32(0.0)).astype(jnp.bfloat16)


def reference(edge_state, angle_weight, angle_bins, send_slots, fetch_index, down_weight, bilinear, up_weight, first_dense, second_dense):
    reverse, live_edge = reverse_table(send_slots, fetch_index)
    edge_rows = edge_state
    for section_index in range(BLOCKS):
        projected = per_brick(partial(project_down, down_l=down_weight[section_index]), edge_rows)
        gathered = fetch_rows(projected, reverse, live_edge)
        lifted = per_brick(partial(triplets, bilinear_l=bilinear[section_index], up_l=up_weight[section_index]), gathered, angle_weight, angle_bins, live_edge)
        returned = fetch_rows(lifted, reverse, live_edge)
        edge_rows = per_brick(partial(residual, first_l=first_dense[section_index], second_l=second_dense[section_index]), edge_rows, returned, live_edge)
    return edge_rows
```

```python
import functools

import jax
import jax.numpy as jnp
from jax import lax
from jax.experimental import pallas as pl
from jax.experimental.pallas import tpu as pltpu
from jax.sharding import PartitionSpec as P

MESH = pl.DeviceIdType.MESH
HALF_ROOT = 0.7071067811865476
BF = jnp.bfloat16
F32 = jnp.float32
LANES = 128
CHUNK = 256


def silu(v):
    h = v * 0.5
    return h + h * jnp.tanh(h)


def place(t):
    if t < 13:
        return t, 0
    return (t - 18, 1) if t >= 18 else (t - 5, 1)


def dot(a, b):
    return jnp.dot(a, b, preferred_element_type=F32)


def kernel(
    sizes,
    rows_hbm,
    weight_hbm,
    bins_hbm,
    send_hbm,
    fetch_hbm,
    down_hbm,
    bilinear_hbm,
    up_hbm,
    first_hbm,
    second_hbm,
    out_hbm,
    rows,
    weight_in,
    bins_in,
    send_in,
    fetch_in,
    down_in,
    bilinear_in,
    up_in,
    first,
    second,
    down2,
    wide,
    up4,
    pick,
    pick_mask,
    send_pick,
    send_mask,
    live,
    nearby,
    coef,
    twice,
    table,
    packed,
    lifted_h,
    send_buf,
    recv_buf,
    in_sem,
    out_sem,
    send_sem,
    recv_sem,
):
    bx, by, bz, trip, slots = sizes
    edges, width = rows.shape
    quarter = edges // 4
    half_slots = slots // 2
    neigh = weight_in.shape[0]
    blocks = down_in.shape[0]
    angular = bilinear_in.shape[2] // trip
    pairs = angular // 2
    shift_quarter = quarter.bit_length() - 1
    shift_slots = slots.bit_length() - 1
    me = (lax.axis_index("gx"), lax.axis_index("gy"), lax.axis_index("gz"))

    loads = []
    for source, target in (
        (send_hbm, send_in),
        (fetch_hbm, fetch_in),
        (down_hbm, down_in),
        (rows_hbm, rows),
        (weight_hbm, weight_in),
        (bins_hbm, bins_in),
        (bilinear_hbm, bilinear_in),
        (up_hbm, up_in),
        (first_hbm, first),
        (second_hbm, second),
    ):
        loads.append(pltpu.make_async_copy(source, target, in_sem.at[len(loads)]))
        loads[-1].start()

    def neighbour(t):
        a, b, c = t // 9 - 1, t // 3 % 3 - 1, t % 3 - 1
        return (
            lax.rem(me[0] + (a + bx), bx),
            lax.rem(me[1] + (b + by), by),
            lax.rem(me[2] + (c + bz), bz),
        )

    parcels = []
    for t in range(27):
        if t == 13:
            continue
        block, half = place(26 - t)
        if bx == 2 and t // 9 != 1:
            if t < 9:
                parcels.append((t, block, 0, 2 * LANES))
        else:
            parcels.append((t, block, half * LANES, LANES))

    barrier = pltpu.get_barrier_semaphore()
    for t, _, _, _ in parcels:
        pl.semaphore_signal(barrier, inc=1, device_id=neighbour(t), device_id_type=MESH)

    lane = lax.broadcasted_iota(jnp.int32, (LANES, LANES), 1)
    sub = lax.broadcasted_iota(jnp.int32, (LANES, LANES), 0)

    def column(ref, i):
        return jnp.broadcast_to(ref[pl.ds(i, 1), :], (LANES, LANES)).T

    def ones_where(mask):
        return jnp.where(mask, F32(1), F32(0)).astype(BF)

    loads[0].wait()
    for i in range(send_pick.shape[0] // LANES):
        at = pl.ds(i * LANES, LANES)
        s = column(send_in, i)
        q = lax.shift_right_arithmetic(s, shift_quarter)
        k = jnp.where(s >= 0, s - q * quarter, -1)
        for m in range(quarter // LANES):
            send_pick[at, pl.ds(m * LANES, LANES)] = ones_where(k == lane + m * LANES)
        for m in range(2):
            send_mask[at, pl.ds(m * LANES, LANES)] = ones_where(
                q == 2 * m + lax.shift_right_logical(lane, 6)
            )
    low = lax.broadcasted_iota(jnp.int32, (half_slots, LANES), 1) < trip
    tail = recv_buf.shape[1] - 13 * half_slots
    for x in range(2 * blocks):
        recv_buf[x, pl.ds(13 * half_slots, tail), :] = jnp.zeros((tail, 2 * LANES), BF)

    loads[2].wait()
    for l in range(blocks):
        turned = down_in[l].astype(F32)
        down2[l] = jnp.concatenate([turned, turned], axis=0).T.astype(BF)
    loads[3].wait()

    def project(l, data):
        return silu(dot(data, down2[l])).astype(BF)

    def each_chunk(body):
        def run(i, carry):
            body(pl.multiple_of(i * CHUNK, CHUNK), i)
            return carry

        lax.fori_loop(0, edges // CHUNK, run, 0)

    def start_exchange(x):
        first_half = lax.broadcasted_iota(jnp.int32, (1, LANES), 1) < trip
        keep_low = ones_where(first_half)
        keep_high = ones_where(jnp.logical_not(first_half))
        for m in range(2):
            table[:, pl.ds(m * LANES, LANES)] = (
                twice[pl.ds(2 * m * quarter, quarter), :] * keep_low
                + twice[pl.ds((2 * m + 1) * quarter, quarter), :] * keep_high
            )
        for i in range(send_pick.shape[0] // LANES):
            at = pl.ds(i * LANES, LANES)
            found = dot(send_pick[at, :], table[...]).astype(BF) * send_mask[at, :]
            folded = found[:, :LANES].astype(F32) + found[:, LANES:].astype(F32)
            packed[at, :] = folded + pltpu.roll(folded, trip, 1)
        for t in range(27):
            if t == 13:
                continue
            block, half = place(26 - t)
            send_buf[x, pl.ds(block * half_slots, half_slots), pl.ds(half * LANES, LANES)] = jnp.where(
                low,
                packed[pl.ds(t * slots, half_slots), :],
                packed[pl.ds(t * slots + half_slots, half_slots), :],
            ).astype(BF)
        if x == 0:
            pl.semaphore_wait(barrier, len(parcels))
        copies = []
        for i, (t, block, at, count) in enumerate(parcels):
            where = (x, pl.ds(block * half_slots, half_slots), pl.ds(at, count))
            copies.append(
                pltpu.make_async_remote_copy(
                    src_ref=send_buf.at[where],
                    dst_ref=recv_buf.at[where],
                    send_sem=send_sem.at[x, i],
                    recv_sem=recv_sem.at[x, i],
                    device_id=neighbour(t),
                    device_id_type=MESH,
                )
            )
            copies[-1].start()
        return copies

    def find_nearby():
        def body(at, i):
            nearby[pl.ds(at, CHUNK), :] = dot(
                pick[pl.ds(at, CHUNK), pl.ds(0, quarter)], table[...]
            ).astype(BF)

        each_chunk(body)

    def reverse_rows(x, at):
        here = pl.ds(at, CHUNK)
        far = dot(pick[here, pl.ds(quarter, 2 * LANES)], recv_buf[x]).astype(BF)
        return (nearby[here, :] + far) * pick_mask[here, :]

    def prepare():
        loads[1].wait()
        loads[4].wait()
        loads[5].wait()

        def body(i, carry):
            at = pl.multiple_of(i * LANES, LANES)
            here = pl.ds(at, LANES)
            f = column(fetch_in, i)
            g = f - edges
            far = g >= 0
            t = lax.shift_right_arithmetic(g, shift_slots)
            r = g - t * slots
            upper = (t > 13).astype(jnp.int32)
            block = t - upper * jnp.where(t >= 18, 18, 5)
            side = lax.shift_right_arithmetic(r, shift_slots - 1)
            q_near = lax.shift_right_arithmetic(f, shift_quarter)
            k_far = quarter + block * half_slots + r - side * half_slots
            q = jnp.where(far, 2 * upper + side, q_near)
            k = jnp.where(far, k_far, jnp.where(f >= 0, f - q_near * quarter, -1))
            for m in range(pick.shape[1] // LANES):
                pick[here, pl.ds(m * LANES, LANES)] = ones_where(k == lane + m * LANES)
            for m in range(2):
                pick_mask[here, pl.ds(m * LANES, LANES)] = ones_where(
                    q == 2 * m + lax.shift_right_logical(lane, 6)
                )
            live[here, :] = jnp.where(f >= 0, F32(1), F32(0))
            copies = LANES // neigh
            w = weight_in[:, here]
            w = jnp.concatenate([w] * copies, axis=0).T
            n = bins_in[:, here]
            n = jnp.concatenate([n] * copies, axis=0).T
            own = (lane & (neigh - 1)) == (sub & (neigh - 1))
            w = jnp.where(own, F32(0), w)
            group = lax.shift_right_logical(lane, neigh.bit_length() - 1)
            for parity in range(2):
                for m in range(pairs // copies):
                    value = jnp.where(n == 2 * (m * copies + group) + parity, w, F32(0)).astype(BF)
                    for a in range(copies):
                        coef[
                            i * copies + a, pl.ds(parity * neigh, neigh), pl.ds(m * LANES, LANES)
                        ] = value[a * neigh : (a + 1) * neigh, :]
            return carry

        lax.fori_loop(0, edges // LANES, body, 0)
        loads[6].wait()
        loads[7].wait()
        for l in range(blocks):
            for p in range(pairs):
                turned = bilinear_in[l, :, pl.ds(p * LANES, LANES)].astype(F32).T
                both = jnp.concatenate([turned[:trip], turned[trip:]], axis=1).astype(BF)
                for q in range(4):
                    wide[l, pl.ds(q * trip, trip), pl.ds(p * LANES, LANES)] = both
            for q in range(4):
                up4[l, pl.ds(q * trip, trip), :] = up_in[l]

    first_lanes = lax.broadcasted_iota(jnp.int32, (neigh, LANES), 1) < trip

    def triplets(l, x):
        def body(at, i):
            lifted_h[...] = dot(reverse_rows(x, at), wide[l]).astype(BF)
            atoms = CHUNK // neigh
            for a in range(atoms):
                stacked = jnp.concatenate(
                    [lifted_h[pl.ds(a * neigh, neigh), pl.ds(p * LANES, LANES)] for p in range(pairs)],
                    axis=0,
                )
                both = dot(coef[i * atoms + a], stacked)
                chosen = jnp.where(first_lanes, both[:neigh], both[neigh:])
                twice[pl.ds(at + a * neigh, neigh), :] = (
                    chosen + pltpu.roll(chosen, trip, 1)
                ).astype(BF)

        each_chunk(body)

    def residual(l, x):
        def body(at, i):
            here = pl.ds(at, CHUNK)
            lifted = silu(dot(reverse_rows(x, at), up4[l])).astype(BF)
            mixed = ((rows[here, :].astype(F32) + lifted.astype(F32)) * HALF_ROOT).astype(BF)
            inner = silu(dot(mixed, first[l])).astype(BF)
            updated = (mixed.astype(F32) + silu(dot(inner, second[l]))) * HALF_ROOT
            alive = jnp.concatenate([live[here, :]] * (width // LANES), axis=1)
            done = jnp.where(alive > 0, updated, F32(0)).astype(BF)
            rows[here, :] = done
            if l + 1 < blocks:
                twice[here, :] = project(l + 1, done)
            else:
                pltpu.make_async_copy(rows.at[here], out_hbm.at[here], out_sem.at[i]).start()

        each_chunk(body)

    def first_project(at, i):
        twice[pl.ds(at, CHUNK), :] = project(0, rows[pl.ds(at, CHUNK), :])

    each_chunk(first_project)
    for l in range(blocks):
        copies = start_exchange(2 * l)
        if l == 0:
            prepare()
        find_nearby()
        for copy in copies:
            copy.wait()
        triplets(l, 2 * l)
        copies = start_exchange(2 * l + 1)
        find_nearby()
        if l == 0:
            loads[8].wait()
            loads[9].wait()
        for copy in copies:
            copy.wait()
        residual(l, 2 * l + 1)

    def finish(at, i):
        here = pl.ds(at, CHUNK)
        pltpu.make_async_copy(rows.at[here], out_hbm.at[here], out_sem.at[i]).wait()

    each_chunk(finish)


def solution(mesh):
    shape = mesh.shape

    def local(
        edge_state,
        angle_weight,
        angle_bins,
        send_slots,
        fetch_index,
        down_weight,
        bilinear,
        up_weight,
        first_dense,
        second_dense,
    ):
        edges, width = edge_state.shape
        neigh = angle_weight.shape[1]
        blocks, _, trip = down_weight.shape
        angular = bilinear.shape[1] // trip
        slots = send_slots.shape[-1]
        quarter = edges // 4
        senders = -(-27 * slots // LANES) * LANES
        listed = jnp.pad(
            send_slots.reshape(27 * slots), (0, senders - 27 * slots), constant_values=-1
        ).reshape(senders // LANES, LANES)
        depth = 2 * LANES
        sizes = (shape["gx"], shape["gy"], shape["gz"], trip, slots)
        parcels = 17 if shape["gx"] == 2 else 26
        exchange = pltpu.VMEM((2 * blocks, depth, 2 * LANES), BF)
        return pl.pallas_call(
            functools.partial(kernel, sizes),
            out_shape=jax.ShapeDtypeStruct((edges, width), BF),
            in_specs=[pl.BlockSpec(memory_space=pl.ANY)] * 10,
            out_specs=pl.BlockSpec(memory_space=pl.ANY),
            scratch_shapes=[
                pltpu.VMEM((edges, width), BF),
                pltpu.VMEM((neigh, edges), F32),
                pltpu.VMEM((neigh, edges), jnp.int32),
                pltpu.VMEM((senders // LANES, LANES), jnp.int32),
                pltpu.VMEM((edges // LANES, LANES), jnp.int32),
                pltpu.VMEM((blocks, trip, width), BF),
                pltpu.VMEM((blocks, trip, angular * trip), BF),
                pltpu.VMEM((blocks, trip, width), BF),
                pltpu.VMEM((blocks, width, width), BF),
                pltpu.VMEM((blocks, width, width), BF),
                pltpu.VMEM((blocks, width, LANES), BF),
                pltpu.VMEM((blocks, 4 * trip, angular * trip), BF),
                pltpu.VMEM((blocks, 4 * trip, width), BF),
                pltpu.VMEM((edges, quarter + depth), BF),
                pltpu.VMEM((edges, 2 * LANES), BF),
                pltpu.VMEM((senders, quarter), BF),
                pltpu.VMEM((senders, 2 * LANES), BF),
                pltpu.VMEM((edges, LANES), F32),
                pltpu.VMEM((edges, 2 * LANES), BF),
                pltpu.VMEM((edges // neigh, 2 * neigh, angular // 2 * neigh), BF),
                pltpu.VMEM((edges, LANES), BF),
                pltpu.VMEM((quarter, 2 * LANES), BF),
                pltpu.VMEM((senders, LANES), F32),
                pltpu.VMEM((CHUNK, angular * trip), BF),
                exchange,
                exchange,
                pltpu.SemaphoreType.DMA((10,)),
                pltpu.SemaphoreType.DMA((edges // CHUNK,)),
                pltpu.SemaphoreType.DMA((2 * blocks, parcels)),
                pltpu.SemaphoreType.DMA((2 * blocks, parcels)),
            ],
            compiler_params=pltpu.CompilerParams(
                collective_id=0, has_side_effects=True, vmem_limit_bytes=48 * 1024 * 1024
            ),
        )(
            edge_state,
            angle_weight.T,
            angle_bins.T,
            listed,
            fetch_index.reshape(edges // LANES, LANES),
            jnp.swapaxes(down_weight, 1, 2),
            jnp.swapaxes(bilinear, 1, 2),
            up_weight,
            first_dense,
            second_dense,
        )

    in_specs = (
        P(("gx", "gy", "gz"), None),
        P(("gx", "gy", "gz"), None),
        P(("gx", "gy", "gz"), None),
        P("gx", "gy", "gz", None, None),
        P(("gx", "gy", "gz")),
        P(),
        P(),
        P(),
        P(),
        P(),
    )
    out_specs = P(("gx", "gy", "gz"), None)
    return jax.shard_map(local, mesh=mesh, in_specs=in_specs, out_specs=out_specs, check_vma=False)
```

```python
import functools

import jax
import jax.numpy as jnp
from jax import lax
from jax.experimental import pallas as pl
from jax.experimental.pallas import tpu as pltpu
from jax.sharding import PartitionSpec as P

MESH = pl.DeviceIdType.MESH
HALF_ROOT = 0.7071067811865476
BF = jnp.bfloat16
F32 = jnp.float32
LANES = 128
CHUNK = 1024


def silu(v):
    h = v.astype(BF) * BF(0.5)
    return h + h * jnp.tanh(h)


def place(t):
    if t < 13:
        return t, 0
    return (t - 18, 1) if t >= 18 else (t - 5, 1)


def dot(a, b):
    return jnp.dot(a, b, preferred_element_type=F32)


def kernel(
    sizes,
    rows_hbm,
    weight_hbm,
    bins_hbm,
    send_hbm,
    fetch_hbm,
    down_hbm,
    bilinear_hbm,
    up_hbm,
    first_hbm,
    second_hbm,
    out_hbm,
    rows,
    weight_in,
    bins_in,
    send_in,
    fetch_in,
    down_in,
    bilinear_in,
    up_in,
    first,
    second,
    down2,
    wide,
    up4,
    pick,
    pick_mask,
    send_pick,
    send_mask,
    live,
    nearby,
    coef,
    twice,
    table,
    packed,
    lifted_h,
    send_buf,
    recv_buf,
    in_sem,
    out_sem,
    send_sem,
    recv_sem,
):
    bx, by, bz, trip, slots = sizes
    edges, width = rows.shape
    quarter = edges // 4
    half_slots = slots // 2
    neigh = weight_in.shape[0]
    blocks = down_in.shape[0]
    angular = bilinear_in.shape[2] // trip
    pairs = angular // 2
    shift_quarter = quarter.bit_length() - 1
    shift_slots = slots.bit_length() - 1
    me = (lax.axis_index("gx"), lax.axis_index("gy"), lax.axis_index("gz"))

    loads = []
    for source, target in (
        (send_hbm, send_in),
        (fetch_hbm, fetch_in),
        (down_hbm, down_in),
        (rows_hbm, rows),
        (weight_hbm, weight_in),
        (bins_hbm, bins_in),
        (bilinear_hbm, bilinear_in),
        (up_hbm, up_in),
        (first_hbm, first),
        (second_hbm, second),
    ):
        loads.append(pltpu.make_async_copy(source, target, in_sem.at[len(loads)]))
        loads[-1].start()

    def neighbour(t):
        a, b, c = t // 9 - 1, t // 3 % 3 - 1, t % 3 - 1
        return (
            lax.rem(me[0] + (a + bx), bx),
            lax.rem(me[1] + (b + by), by),
            lax.rem(me[2] + (c + bz), bz),
        )

    parcels = []
    for t in range(27):
        if t == 13:
            continue
        block, half = place(26 - t)
        if bx == 2 and t // 9 != 1:
            if t < 9:
                parcels.append((t, block, 0, 2 * LANES))
        else:
            parcels.append((t, block, half * LANES, LANES))

    barrier = pltpu.get_barrier_semaphore()
    for t, _, _, _ in parcels:
        pl.semaphore_signal(barrier, inc=1, device_id=neighbour(t), device_id_type=MESH)

    lane = lax.broadcasted_iota(jnp.int32, (LANES, LANES), 1)
    sub = lax.broadcasted_iota(jnp.int32, (LANES, LANES), 0)

    def column(ref, i):
        return jnp.broadcast_to(ref[pl.ds(i, 1), :], (LANES, LANES)).T

    def ones_where(mask):
        return jnp.where(mask, F32(1), F32(0)).astype(BF)

    loads[0].wait()
    for i in range(send_pick.shape[0] // LANES):
        at = pl.ds(i * LANES, LANES)
        s = column(send_in, i)
        q = lax.shift_right_arithmetic(s, shift_quarter)
        k = jnp.where(s >= 0, s - q * quarter, -1)
        for m in range(quarter // LANES):
            send_pick[at, pl.ds(m * LANES, LANES)] = ones_where(k == lane + m * LANES)
        for m in range(2):
            send_mask[at, pl.ds(m * LANES, LANES)] = ones_where(
                q == 2 * m + lax.shift_right_logical(lane, 6)
            )
    low = lax.broadcasted_iota(jnp.int32, (half_slots, LANES), 1) < trip
    tail = recv_buf.shape[1] - 13 * half_slots
    for x in range(2 * blocks):
        recv_buf[x, pl.ds(13 * half_slots, tail), :] = jnp.zeros((tail, 2 * LANES), BF)

    loads[2].wait()
    for l in range(blocks):
        turned = down_in[l].astype(F32)
        down2[l] = jnp.concatenate([turned, turned], axis=0).T.astype(BF)
    loads[3].wait()

    def project(l, data):
        return silu(dot(data, down2[l]))

    def each_chunk(body):
        def run(i, carry):
            body(pl.multiple_of(i * CHUNK, CHUNK), i)
            return carry

        lax.fori_loop(0, edges // CHUNK, run, 0)

    def start_exchange(x):
        first_half = lax.broadcasted_iota(jnp.int32, (1, LANES), 1) < trip
        keep_low = ones_where(first_half)
        keep_high = ones_where(jnp.logical_not(first_half))
        for m in range(2):
            table[:, pl.ds(m * LANES, LANES)] = (
                twice[pl.ds(2 * m * quarter, quarter), :] * keep_low
                + twice[pl.ds((2 * m + 1) * quarter, quarter), :] * keep_high
            )
        for i in range(send_pick.shape[0] // LANES):
            at = pl.ds(i * LANES, LANES)
            found = dot(send_pick[at, :], table[...]).astype(BF) * send_mask[at, :]
            folded = found[:, :LANES].astype(F32) + found[:, LANES:].astype(F32)
            packed[at, :] = folded + pltpu.roll(folded, trip, 1)
        for t in range(27):
            if t == 13:
                continue
            block, half = place(26 - t)
            send_buf[x, pl.ds(block * half_slots, half_slots), pl.ds(half * LANES, LANES)] = jnp.where(
                low,
                packed[pl.ds(t * slots, half_slots), :],
                packed[pl.ds(t * slots + half_slots, half_slots), :],
            ).astype(BF)
        if x == 0:
            pl.semaphore_wait(barrier, len(parcels))
        copies = []
        for i, (t, block, at, count) in enumerate(parcels):
            where = (x, pl.ds(block * half_slots, half_slots), pl.ds(at, count))
            copies.append(
                pltpu.make_async_remote_copy(
                    src_ref=send_buf.at[where],
                    dst_ref=recv_buf.at[where],
                    send_sem=send_sem.at[x, i],
                    recv_sem=recv_sem.at[x, i],
                    device_id=neighbour(t),
                    device_id_type=MESH,
                )
            )
            copies[-1].start()
        return copies

    def find_nearby():
        def body(at, i):
            nearby[pl.ds(at, CHUNK), :] = dot(
                pick[pl.ds(at, CHUNK), pl.ds(0, quarter)], table[...]
            ).astype(BF)

        each_chunk(body)

    def reverse_rows(x, at):
        here = pl.ds(at, CHUNK)
        far = dot(pick[here, pl.ds(quarter, 2 * LANES)], recv_buf[x]).astype(BF)
        return (nearby[here, :] + far) * pick_mask[here, :]

    def prepare():
        loads[1].wait()
        loads[4].wait()
        loads[5].wait()

        def body(i, carry):
            at = pl.multiple_of(i * LANES, LANES)
            here = pl.ds(at, LANES)
            f = column(fetch_in, i)
            g = f - edges
            far = g >= 0
            t = lax.shift_right_arithmetic(g, shift_slots)
            r = g - t * slots
            upper = (t > 13).astype(jnp.int32)
            block = t - upper * jnp.where(t >= 18, 18, 5)
            side = lax.shift_right_arithmetic(r, shift_slots - 1)
            q_near = lax.shift_right_arithmetic(f, shift_quarter)
            k_far = quarter + block * half_slots + r - side * half_slots
            q = jnp.where(far, 2 * upper + side, q_near)
            k = jnp.where(far, k_far, jnp.where(f >= 0, f - q_near * quarter, -1))
            for m in range(pick.shape[1] // LANES):
                pick[here, pl.ds(m * LANES, LANES)] = ones_where(k == lane + m * LANES)
            for m in range(2):
                pick_mask[here, pl.ds(m * LANES, LANES)] = ones_where(
                    q == 2 * m + lax.shift_right_logical(lane, 6)
                )
            live[here, :] = jnp.where(f >= 0, F32(1), F32(0))
            copies = LANES // neigh
            w = weight_in[:, here]
            w = jnp.concatenate([w] * copies, axis=0).T
            n = bins_in[:, here]
            n = jnp.concatenate([n] * copies, axis=0).T
            own = (lane & (neigh - 1)) == (sub & (neigh - 1))
            w = jnp.where(own, F32(0), w)
            group = lax.shift_right_logical(lane, neigh.bit_length() - 1)
            for parity in range(2):
                for m in range(pairs // copies):
                    value = jnp.where(n == 2 * (m * copies + group) + parity, w, F32(0)).astype(BF)
                    for a in range(copies):
                        coef[
                            i * copies + a, pl.ds(parity * neigh, neigh), pl.ds(m * LANES, LANES)
                        ] = value[a * neigh : (a + 1) * neigh, :]
            return carry

        lax.fori_loop(0, edges // LANES, body, 0)
        loads[6].wait()
        loads[7].wait()
        for l in range(blocks):
            for p in range(pairs):
                turned = bilinear_in[l, :, pl.ds(p * LANES, LANES)].astype(F32).T
                both = jnp.concatenate([turned[:trip], turned[trip:]], axis=1).astype(BF)
                for q in range(4):
                    wide[l, pl.ds(q * trip, trip), pl.ds(p * LANES, LANES)] = both
            for q in range(4):
                up4[l, pl.ds(q * trip, trip), :] = up_in[l]

    first_lanes = lax.broadcasted_iota(jnp.int32, (neigh, LANES), 1) < trip

    def triplets(l, x):
        def body(at, i):
            lifted_h[...] = dot(reverse_rows(x, at), wide[l]).astype(BF)
            atoms = CHUNK // neigh
            for a in range(atoms):
                stacked = jnp.concatenate(
                    [lifted_h[pl.ds(a * neigh, neigh), pl.ds(p * LANES, LANES)] for p in range(pairs)],
                    axis=0,
                )
                both = dot(coef[i * atoms + a], stacked)
                chosen = jnp.where(first_lanes, both[:neigh], both[neigh:])
                twice[pl.ds(at + a * neigh, neigh), :] = (
                    chosen + pltpu.roll(chosen, trip, 1)
                ).astype(BF)

        each_chunk(body)

    def residual(l, x):
        def body(at, i):
            here = pl.ds(at, CHUNK)
            lifted = silu(dot(reverse_rows(x, at), up4[l]))
            mixed = ((rows[here, :].astype(F32) + lifted.astype(F32)) * HALF_ROOT).astype(BF)
            inner = silu(dot(mixed, first[l]))
            updated = (mixed.astype(F32) + silu(dot(inner, second[l])).astype(F32)) * HALF_ROOT
            alive = jnp.concatenate([live[here, :]] * (width // LANES), axis=1)
            done = jnp.where(alive > 0, updated, F32(0)).astype(BF)
            rows[here, :] = done
            if l + 1 < blocks:
                twice[here, :] = project(l + 1, done)
            else:
                pltpu.make_async_copy(rows.at[here], out_hbm.at[here], out_sem.at[i]).start()

        each_chunk(body)

    def first_project(at, i):
        twice[pl.ds(at, CHUNK), :] = project(0, rows[pl.ds(at, CHUNK), :])

    each_chunk(first_project)
    for l in range(blocks):
        copies = start_exchange(2 * l)
        if l == 0:
            prepare()
        find_nearby()
        for copy in copies:
            copy.wait()
        triplets(l, 2 * l)
        copies = start_exchange(2 * l + 1)
        find_nearby()
        if l == 0:
            loads[8].wait()
            loads[9].wait()
        for copy in copies:
            copy.wait()
        residual(l, 2 * l + 1)

    def finish(at, i):
        here = pl.ds(at, CHUNK)
        pltpu.make_async_copy(rows.at[here], out_hbm.at[here], out_sem.at[i]).wait()

    each_chunk(finish)


def solution(mesh):
    shape = mesh.shape

    def local(
        edge_state,
        angle_weight,
        angle_bins,
        send_slots,
        fetch_index,
        down_weight,
        bilinear,
        up_weight,
        first_dense,
        second_dense,
    ):
        edges, width = edge_state.shape
        neigh = angle_weight.shape[1]
        blocks, _, trip = down_weight.shape
        angular = bilinear.shape[1] // trip
        slots = send_slots.shape[-1]
        quarter = edges // 4
        senders = -(-27 * slots // LANES) * LANES
        listed = jnp.pad(
            send_slots.reshape(27 * slots), (0, senders - 27 * slots), constant_values=-1
        ).reshape(senders // LANES, LANES)
        depth = 2 * LANES
        sizes = (shape["gx"], shape["gy"], shape["gz"], trip, slots)
        parcels = 17 if shape["gx"] == 2 else 26
        exchange = pltpu.VMEM((2 * blocks, depth, 2 * LANES), BF)
        return pl.pallas_call(
            functools.partial(kernel, sizes),
            out_shape=jax.ShapeDtypeStruct((edges, width), BF),
            in_specs=[pl.BlockSpec(memory_space=pl.ANY)] * 10,
            out_specs=pl.BlockSpec(memory_space=pl.ANY),
            scratch_shapes=[
                pltpu.VMEM((edges, width), BF),
                pltpu.VMEM((neigh, edges), F32),
                pltpu.VMEM((neigh, edges), jnp.int32),
                pltpu.VMEM((senders // LANES, LANES), jnp.int32),
                pltpu.VMEM((edges // LANES, LANES), jnp.int32),
                pltpu.VMEM((blocks, trip, width), BF),
                pltpu.VMEM((blocks, trip, angular * trip), BF),
                pltpu.VMEM((blocks, trip, width), BF),
                pltpu.VMEM((blocks, width, width), BF),
                pltpu.VMEM((blocks, width, width), BF),
                pltpu.VMEM((blocks, width, LANES), BF),
                pltpu.VMEM((blocks, 4 * trip, angular * trip), BF),
                pltpu.VMEM((blocks, 4 * trip, width), BF),
                pltpu.VMEM((edges, quarter + depth), BF),
                pltpu.VMEM((edges, 2 * LANES), BF),
                pltpu.VMEM((senders, quarter), BF),
                pltpu.VMEM((senders, 2 * LANES), BF),
                pltpu.VMEM((edges, LANES), F32),
                pltpu.VMEM((edges, 2 * LANES), BF),
                pltpu.VMEM((edges // neigh, 2 * neigh, angular // 2 * neigh), BF),
                pltpu.VMEM((edges, LANES), BF),
                pltpu.VMEM((quarter, 2 * LANES), BF),
                pltpu.VMEM((senders, LANES), F32),
                pltpu.VMEM((CHUNK, angular * trip), BF),
                exchange,
                exchange,
                pltpu.SemaphoreType.DMA((10,)),
                pltpu.SemaphoreType.DMA((edges // CHUNK,)),
                pltpu.SemaphoreType.DMA((2 * blocks, parcels)),
                pltpu.SemaphoreType.DMA((2 * blocks, parcels)),
            ],
            compiler_params=pltpu.CompilerParams(
                collective_id=0, has_side_effects=True, vmem_limit_bytes=60 * 1024 * 1024
            ),
        )(
            edge_state,
            angle_weight.T,
            angle_bins.T,
            listed,
            fetch_index.reshape(edges // LANES, LANES),
            jnp.swapaxes(down_weight, 1, 2),
            jnp.swapaxes(bilinear, 1, 2),
            up_weight,
            first_dense,
            second_dense,
        )

    in_specs = (
        P(("gx", "gy", "gz"), None),
        P(("gx", "gy", "gz"), None),
        P(("gx", "gy", "gz"), None),
        P("gx", "gy", "gz", None, None),
        P(("gx", "gy", "gz")),
        P(),
        P(),
        P(),
        P(),
        P(),
    )
    out_specs = P(("gx", "gy", "gz"), None)
    return jax.shard_map(local, mesh=mesh, in_specs=in_specs, out_specs=out_specs, check_vma=False)
```

```python
import functools

import jax
import jax.numpy as jnp
from jax import lax
from jax.experimental import pallas as pl
from jax.experimental.pallas import tpu as pltpu
from jax.sharding import PartitionSpec as P

MESH = pl.DeviceIdType.MESH
HALF_ROOT = 0.7071067811865476
BF = jnp.bfloat16
F32 = jnp.float32
LANES = 128
CHUNK = 1024


def silu(v):
    h = v.astype(BF) * BF(0.5)
    return h + h * jnp.tanh(h)


def place(t):
    if t < 13:
        return t, 0
    return (t - 18, 1) if t >= 18 else (t - 5, 1)


def dot(a, b):
    return jnp.dot(a, b, preferred_element_type=F32)


def kernel(
    sizes,
    rows_hbm,
    weight_hbm,
    bins_hbm,
    send_hbm,
    fetch_hbm,
    down_hbm,
    bilinear_hbm,
    up_hbm,
    first_hbm,
    second_hbm,
    out_hbm,
    rows,
    weight_in,
    bins_in,
    send_in,
    fetch_in,
    down_in,
    bilinear_in,
    up_in,
    first,
    second,
    down2,
    wide,
    up4,
    pick,
    pick_mask,
    send_pick,
    send_mask,
    live,
    nearby,
    coef,
    twice,
    table,
    packed,
    lifted_h,
    send_buf,
    recv_buf,
    in_sem,
    out_sem,
    send_sem,
    recv_sem,
):
    bx, by, bz, trip, slots = sizes
    edges, width = rows.shape
    quarter = edges // 4
    half_slots = slots // 2
    neigh = weight_in.shape[0]
    blocks = down_in.shape[0]
    angular = bilinear_in.shape[2] // trip
    pairs = angular // 2
    shift_quarter = quarter.bit_length() - 1
    shift_slots = slots.bit_length() - 1
    me = (lax.axis_index("gx"), lax.axis_index("gy"), lax.axis_index("gz"))

    loads = []
    for source, target in (
        (send_hbm, send_in),
        (fetch_hbm, fetch_in),
        (down_hbm, down_in),
        (rows_hbm, rows),
        (weight_hbm, weight_in),
        (bins_hbm, bins_in),
        (bilinear_hbm, bilinear_in),
        (up_hbm, up_in),
        (first_hbm, first),
        (second_hbm, second),
    ):
        loads.append(pltpu.make_async_copy(source, target, in_sem.at[len(loads)]))
        loads[-1].start()

    def neighbour(t):
        a, b, c = t // 9 - 1, t // 3 % 3 - 1, t % 3 - 1
        return (
            lax.rem(me[0] + (a + bx), bx),
            lax.rem(me[1] + (b + by), by),
            lax.rem(me[2] + (c + bz), bz),
        )

    parcels = []
    for t in range(27):
        if t == 13:
            continue
        block, half = place(26 - t)
        if bx == 2 and t // 9 != 1:
            if t < 9:
                parcels.append((t, block, 0, 2 * LANES))
        else:
            parcels.append((t, block, half * LANES, LANES))

    barrier = pltpu.get_barrier_semaphore()
    for t, _, _, _ in parcels:
        pl.semaphore_signal(barrier, inc=1, device_id=neighbour(t), device_id_type=MESH)

    lane = lax.broadcasted_iota(jnp.int32, (LANES, LANES), 1)
    sub = lax.broadcasted_iota(jnp.int32, (LANES, LANES), 0)

    def column(ref, i):
        return jnp.broadcast_to(ref[pl.ds(i, 1), :], (LANES, LANES)).T

    def ones_where(mask):
        return jnp.where(mask, F32(1), F32(0)).astype(BF)

    loads[0].wait()
    for i in range(send_pick.shape[0] // LANES):
        at = pl.ds(i * LANES, LANES)
        s = column(send_in, i)
        q = lax.shift_right_arithmetic(s, shift_quarter)
        k = jnp.where(s >= 0, s - q * quarter, -1)
        for m in range(quarter // LANES):
            send_pick[at, pl.ds(m * LANES, LANES)] = ones_where(k == lane + m * LANES)
        for m in range(2):
            send_mask[at, pl.ds(m * LANES, LANES)] = ones_where(
                q == 2 * m + lax.shift_right_logical(lane, 6)
            )
    low = lax.broadcasted_iota(jnp.int32, (half_slots, LANES), 1) < trip
    tail = recv_buf.shape[1] - 13 * half_slots
    for x in range(2 * blocks):
        recv_buf[x, pl.ds(13 * half_slots, tail), :] = jnp.zeros((tail, 2 * LANES), BF)

    loads[2].wait()
    for l in range(blocks):
        turned = down_in[l].astype(F32)
        down2[l] = jnp.concatenate([turned, turned], axis=0).T.astype(BF)
    loads[3].wait()

    def project(l, data):
        return silu(dot(data, down2[l]))

    def each_chunk(body):
        def run(i, carry):
            body(pl.multiple_of(i * CHUNK, CHUNK), i)
            return carry

        lax.fori_loop(0, edges // CHUNK, run, 0)

    def start_exchange(x):
        first_half = lax.broadcasted_iota(jnp.int32, (1, LANES), 1) < trip
        keep_low = ones_where(first_half)
        keep_high = ones_where(jnp.logical_not(first_half))
        for m in range(2):
            table[:, pl.ds(m * LANES, LANES)] = (
                twice[pl.ds(2 * m * quarter, quarter), :] * keep_low
                + twice[pl.ds((2 * m + 1) * quarter, quarter), :] * keep_high
            )
        found = dot(send_pick[...], table[...]).astype(BF) * send_mask[...]
        folded = found[:, :LANES].astype(F32) + found[:, LANES:].astype(F32)
        packed[...] = folded + pltpu.roll(folded, trip, 1)
        for t in range(27):
            if t == 13:
                continue
            block, half = place(26 - t)
            send_buf[x, pl.ds(block * half_slots, half_slots), pl.ds(half * LANES, LANES)] = jnp.where(
                low,
                packed[pl.ds(t * slots, half_slots), :],
                packed[pl.ds(t * slots + half_slots, half_slots), :],
            ).astype(BF)
        if x == 0:
            pl.semaphore_wait(barrier, len(parcels))
        copies = []
        for i, (t, block, at, count) in enumerate(parcels):
            where = (x, pl.ds(block * half_slots, half_slots), pl.ds(at, count))
            copies.append(
                pltpu.make_async_remote_copy(
                    src_ref=send_buf.at[where],
                    dst_ref=recv_buf.at[where],
                    send_sem=send_sem.at[x, i],
                    recv_sem=recv_sem.at[x, i],
                    device_id=neighbour(t),
                    device_id_type=MESH,
                )
            )
            copies[-1].start()
        return copies

    def find_nearby():
        def body(at, i):
            nearby[pl.ds(at, CHUNK), :] = dot(
                pick[pl.ds(at, CHUNK), pl.ds(0, quarter)], table[...]
            ).astype(BF)

        each_chunk(body)

    def reverse_rows(x, at):
        here = pl.ds(at, CHUNK)
        far = dot(pick[here, pl.ds(quarter, 2 * LANES)], recv_buf[x]).astype(BF)
        return (nearby[here, :] + far) * pick_mask[here, :]

    def prepare():
        loads[1].wait()
        loads[4].wait()
        loads[5].wait()

        def body(i, carry):
            at = pl.multiple_of(i * LANES, LANES)
            here = pl.ds(at, LANES)
            f = column(fetch_in, i)
            g = f - edges
            far = g >= 0
            t = lax.shift_right_arithmetic(g, shift_slots)
            r = g - t * slots
            upper = (t > 13).astype(jnp.int32)
            block = t - upper * jnp.where(t >= 18, 18, 5)
            side = lax.shift_right_arithmetic(r, shift_slots - 1)
            q_near = lax.shift_right_arithmetic(f, shift_quarter)
            k_far = quarter + block * half_slots + r - side * half_slots
            q = jnp.where(far, 2 * upper + side, q_near)
            k = jnp.where(far, k_far, jnp.where(f >= 0, f - q_near * quarter, -1))
            for m in range(pick.shape[1] // LANES):
                pick[here, pl.ds(m * LANES, LANES)] = ones_where(k == lane + m * LANES)
            for m in range(2):
                pick_mask[here, pl.ds(m * LANES, LANES)] = ones_where(
                    q == 2 * m + lax.shift_right_logical(lane, 6)
                )
            live[here, :] = jnp.where(f >= 0, F32(1), F32(0))
            copies = LANES // neigh
            w = weight_in[:, here]
            w = jnp.concatenate([w] * copies, axis=0).T
            n = bins_in[:, here]
            n = jnp.concatenate([n] * copies, axis=0).T
            own = (lane & (neigh - 1)) == (sub & (neigh - 1))
            w = jnp.where(own, F32(0), w)
            group = lax.shift_right_logical(lane, neigh.bit_length() - 1)
            for parity in range(2):
                for m in range(pairs // copies):
                    value = jnp.where(n == 2 * (m * copies + group) + parity, w, F32(0)).astype(BF)
                    for a in range(copies):
                        coef[
                            i * copies + a, pl.ds(parity * neigh, neigh), pl.ds(m * LANES, LANES)
                        ] = value[a * neigh : (a + 1) * neigh, :]
            return carry

        lax.fori_loop(0, edges // LANES, body, 0, unroll=4)
        loads[6].wait()
        loads[7].wait()
        for l in range(blocks):
            for p in range(pairs):
                turned = bilinear_in[l, :, pl.ds(p * LANES, LANES)].astype(F32).T
                both = jnp.concatenate([turned[:trip], turned[trip:]], axis=1).astype(BF)
                for q in range(4):
                    wide[l, pl.ds(q * trip, trip), pl.ds(p * LANES, LANES)] = both
            for q in range(4):
                up4[l, pl.ds(q * trip, trip), :] = up_in[l]

    first_lanes = lax.broadcasted_iota(jnp.int32, (neigh, LANES), 1) < trip

    def triplets(l, x):
        def body(at, i):
            lifted_h[...] = dot(reverse_rows(x, at), wide[l]).astype(BF)
            atoms = CHUNK // neigh
            for a in range(atoms):
                stacked = jnp.concatenate(
                    [lifted_h[pl.ds(a * neigh, neigh), pl.ds(p * LANES, LANES)] for p in range(pairs)],
                    axis=0,
                )
                both = dot(coef[i * atoms + a], stacked)
                chosen = jnp.where(first_lanes, both[:neigh], both[neigh:])
                twice[pl.ds(at + a * neigh, neigh), :] = (
                    chosen + pltpu.roll(chosen, trip, 1)
                ).astype(BF)

        each_chunk(body)

    def residual(l, x):
        def body(at, i):
            here = pl.ds(at, CHUNK)
            lifted = silu(dot(reverse_rows(x, at), up4[l]))
            mixed = ((rows[here, :].astype(F32) + lifted.astype(F32)) * HALF_ROOT).astype(BF)
            inner = silu(dot(mixed, first[l]))
            updated = (mixed.astype(F32) + silu(dot(inner, second[l])).astype(F32)) * HALF_ROOT
            alive = jnp.concatenate([live[here, :]] * (width // LANES), axis=1)
            done = jnp.where(alive > 0, updated, F32(0)).astype(BF)
            rows[here, :] = done
            if l + 1 < blocks:
                twice[here, :] = project(l + 1, done)
            else:
                pltpu.make_async_copy(rows.at[here], out_hbm.at[here], out_sem.at[i]).start()

        each_chunk(body)

    def first_project(at, i):
        twice[pl.ds(at, CHUNK), :] = project(0, rows[pl.ds(at, CHUNK), :])

    each_chunk(first_project)
    for l in range(blocks):
        copies = start_exchange(2 * l)
        if l == 0:
            prepare()
        find_nearby()
        for copy in copies:
            copy.wait()
        triplets(l, 2 * l)
        copies = start_exchange(2 * l + 1)
        find_nearby()
        if l == 0:
            loads[8].wait()
            loads[9].wait()
        for copy in copies:
            copy.wait()
        residual(l, 2 * l + 1)

    def finish(at, i):
        here = pl.ds(at, CHUNK)
        pltpu.make_async_copy(rows.at[here], out_hbm.at[here], out_sem.at[i]).wait()

    each_chunk(finish)


def solution(mesh):
    shape = mesh.shape

    def local(
        edge_state,
        angle_weight,
        angle_bins,
        send_slots,
        fetch_index,
        down_weight,
        bilinear,
        up_weight,
        first_dense,
        second_dense,
    ):
        edges, width = edge_state.shape
        neigh = angle_weight.shape[1]
        blocks, _, trip = down_weight.shape
        angular = bilinear.shape[1] // trip
        slots = send_slots.shape[-1]
        quarter = edges // 4
        senders = -(-27 * slots // LANES) * LANES
        listed = jnp.pad(
            send_slots.reshape(27 * slots), (0, senders - 27 * slots), constant_values=-1
        ).reshape(senders // LANES, LANES)
        depth = 2 * LANES
        sizes = (shape["gx"], shape["gy"], shape["gz"], trip, slots)
        parcels = 17 if shape["gx"] == 2 else 26
        exchange = pltpu.VMEM((2 * blocks, depth, 2 * LANES), BF)
        return pl.pallas_call(
            functools.partial(kernel, sizes),
            out_shape=jax.ShapeDtypeStruct((edges, width), BF),
            in_specs=[pl.BlockSpec(memory_space=pl.ANY)] * 10,
            out_specs=pl.BlockSpec(memory_space=pl.ANY),
            scratch_shapes=[
                pltpu.VMEM((edges, width), BF),
                pltpu.VMEM((neigh, edges), F32),
                pltpu.VMEM((neigh, edges), jnp.int32),
                pltpu.VMEM((senders // LANES, LANES), jnp.int32),
                pltpu.VMEM((edges // LANES, LANES), jnp.int32),
                pltpu.VMEM((blocks, trip, width), BF),
                pltpu.VMEM((blocks, trip, angular * trip), BF),
                pltpu.VMEM((blocks, trip, width), BF),
                pltpu.VMEM((blocks, width, width), BF),
                pltpu.VMEM((blocks, width, width), BF),
                pltpu.VMEM((blocks, width, LANES), BF),
                pltpu.VMEM((blocks, 4 * trip, angular * trip), BF),
                pltpu.VMEM((blocks, 4 * trip, width), BF),
                pltpu.VMEM((edges, quarter + depth), BF),
                pltpu.VMEM((edges, 2 * LANES), BF),
                pltpu.VMEM((senders, quarter), BF),
                pltpu.VMEM((senders, 2 * LANES), BF),
                pltpu.VMEM((edges, LANES), F32),
                pltpu.VMEM((edges, 2 * LANES), BF),
                pltpu.VMEM((edges // neigh, 2 * neigh, angular // 2 * neigh), BF),
                pltpu.VMEM((edges, LANES), BF),
                pltpu.VMEM((quarter, 2 * LANES), BF),
                pltpu.VMEM((senders, LANES), F32),
                pltpu.VMEM((CHUNK, angular * trip), BF),
                exchange,
                exchange,
                pltpu.SemaphoreType.DMA((10,)),
                pltpu.SemaphoreType.DMA((edges // CHUNK,)),
                pltpu.SemaphoreType.DMA((2 * blocks, parcels)),
                pltpu.SemaphoreType.DMA((2 * blocks, parcels)),
            ],
            compiler_params=pltpu.CompilerParams(
                collective_id=0, has_side_effects=True, vmem_limit_bytes=60 * 1024 * 1024
            ),
        )(
            edge_state,
            angle_weight.T,
            angle_bins.T,
            listed,
            fetch_index.reshape(edges // LANES, LANES),
            jnp.swapaxes(down_weight, 1, 2),
            jnp.swapaxes(bilinear, 1, 2),
            up_weight,
            first_dense,
            second_dense,
        )

    in_specs = (
        P(("gx", "gy", "gz"), None),
        P(("gx", "gy", "gz"), None),
        P(("gx", "gy", "gz"), None),
        P("gx", "gy", "gz", None, None),
        P(("gx", "gy", "gz")),
        P(),
        P(),
        P(),
        P(),
        P(),
    )
    out_specs = P(("gx", "gy", "gz"), None)
    return jax.shard_map(local, mesh=mesh, in_specs=in_specs, out_specs=out_specs, check_vma=False)
```
